32 devices in a mesh: ep: 16 (over z, y, x), fsdp: 2 (over core).
Axes of the slice: x: 2, y: 2, z: 4, core: 2. Of those that a mesh axis runs over, the one named last changes fastest.
Arguments:
- tokens: bfloat16 [1536, 4096], P(('ep', 'fsdp')), may hold values from -6 to 6
- expert_ids: int32 [1536, 8], P(('ep', 'fsdp')), may hold values from 0 to 15, all different within a row; in each aligned block of 48 rows (0 to 47, 48 to 95, ...) at most 36 rows name the same one
- gate_values: float32 [1536, 8], P(('ep', 'fsdp')), may hold values from 0.05 to 1
- gate_weight: bfloat16 [16, 4096, 1024], P('ep', None, 'fsdp'), may hold values from -0.09375 to 0.09375
- up_weight: bfloat16 [16, 4096, 1024], P('ep', None, 'fsdp'), may hold values from -0.09375 to 0.09375
- down_weight: bfloat16 [16, 4096, 1024], P('ep', None, 'fsdp'), may hold values from -0.1875 to 0.1875
Outputs:
- mixed: bfloat16 [1536, 4096], P(('ep', 'fsdp'))
The draws below stay inside these ranges and needn't reach their ends.
Inputs may be any that keep to these rules, and one draw needn't show every extreme that they name: `expert_ids`: each row names 8 different experts. Among the rows of one device's aligned block of 48 tokens no expert is named more than 36 times, and in some blocks one expert is named exactly 36 times.
All inputs are finite; a program needn't handle non-finite values.
Results may differ from the reference program's by a relative error of at most 0.0057.
Values may be sent and summed in bfloat16 or wider, within the bound.
A program may use at most 128 MiB of HBM per device.

```python
import math
import jax
import jax.numpy as jnp
import numpy as np
from jax import lax

D = 4096
FWIN = 1024
TOPK = 8
TOK_DEV = 48
EXPERTS = 16
CAP = 36
TOKENS = 1536


def levels(stream_key, shape, cuts, smallest, largest):
    factor_of, own = 1.0, jax.random.fold_in(stream_key, 6)
    for position, shards_of in cuts:
        draws = jnp.exp(jax.random.uniform(jax.random.fold_in(own, position), (shards_of,), jnp.float32, smallest / len(cuts), largest / len(cuts)))
        factor_of = factor_of * jnp.repeat(draws, shape[position] // shards_of).reshape([-1 if axis == position else 1 for axis in range(len(shape))])
    return factor_of


def deal_out(key, own, number, rows, count, top, limit, lean):
    ranking = jax.random.permutation(key, count)
    crowded, usual = shares(count, rows * top, limit, lean, True), shares(count, rows * top, limit, lean, False)
    places = jnp.arange(count)

    def named(tallies, offset_by):
        used = int((tallies > 0).sum())
        fixed = max(1, used // 4)
        moved = fixed + (places - fixed + offset_by * (used - fixed)) % max(1, count - fixed)
        return jnp.zeros((count,), jnp.int32).at[ranking[jnp.where(places < fixed, places, moved)]].set(jnp.asarray(tallies, jnp.int32))

    tallies = jnp.where(number % 4 == 0, named(crowded, number // 4), named(usual, number - number // 4 - 1))
    mixed = jax.random.permutation(jax.random.fold_in(own, 3), count)
    donor, receiver = mixed[0:count // 2 * 2:2], mixed[1:count // 2 * 2:2]
    slack = jnp.minimum(tallies[donor] - 1, limit - tallies[receiver]) // 2
    slack = jnp.where((donor == ranking[0]) | (receiver == ranking[0]) | (tallies[receiver] == 0), 0, jnp.maximum(slack, 0))
    moved = jax.random.randint(jax.random.fold_in(own, 4), (count // 2,), 0, 1 << 20) % (slack + 1)
    tallies = tallies.at[donor].add(-moved).at[receiver].add(moved)
    members = jnp.searchsorted(jnp.cumsum(tallies), jnp.arange(rows * top), side="right").astype(jnp.int32)
    table = members.reshape(top, rows).T
    table = table[jax.random.permutation(jax.random.fold_in(own, 1), rows)]
    offset_by = jax.random.randint(jax.random.fold_in(own, 2), (rows, 1), 0, top)
    return jnp.take_along_axis(table, (jnp.arange(top)[None, :] + offset_by) % top, axis=1)


def shares(amount, total, reach, skew, full):
    portions = [(1 << 20) // math.isqrt(grade ** skew) + 1 for grade in range(1, amount + 1)]
    largest = reach if full else min(reach, max(-(-total // amount), total * portions[0] // sum(portions)))
    least = 1 if total - largest >= amount - 1 else 0
    given, spare = [largest] + [least] * (amount - 1), total - largest - least * (amount - 1)
    while spare > 0:
        movable = [i for i in range(1, amount) if given[i] < largest] or [i for i in range(1, amount) if given[i] < reach]
        mass, remaining = sum([portions[i] for i in movable]), spare
        for i in movable:
            more = min(reach - given[i], max(1, remaining * portions[i] // mass), spare)
            given[i] = given[i] + more
            spare = spare - more
    return np.array(given)


def noise(rng, extent, scale, reach, cuts=(), kind=jnp.bfloat16):
    gain = levels(rng, extent, cuts, -0.22, 0.18) if cuts else 1.0
    values = jax.random.normal(rng, extent, jnp.float32) * scale * gain
    return jnp.minimum(jnp.maximum(values, -reach), reach).astype(kind)


def setup_inputs(seed: int = 0) -> dict:
    keys = jax.random.split(jax.random.key(seed), 7)
    tokens = noise(keys[0], (TOKENS, D), 1.0, 6.0, ((0, 32),))
    expert_ids_keys = jax.random.split(jax.random.fold_in(keys[1], 1), TOKENS // TOK_DEV)
    expert_ids_turns = jax.random.permutation(jax.random.fold_in(keys[1], 3), TOKENS // TOK_DEV)
    expert_ids = jax.vmap(lambda own, number: deal_out(jax.random.fold_in(keys[1], 2), own, number, TOK_DEV, EXPERTS, TOPK, CAP, 2))(expert_ids_keys, expert_ids_turns).reshape((TOKENS, TOPK))
    gate_values = jnp.clip(jnp.exp(math.log(1.0) - 2.9957323 * jax.random.uniform(keys[2], (TOKENS, TOPK), jnp.float32) ** levels(keys[2], (TOKENS, TOPK), ((0, 32),), -0.2, 0.2)), 0.05, 1.0)
    gate_weight = noise(keys[3], (EXPERTS, D, FWIN), D ** -0.5, 0.09375, ((0, 16), (2, 2)))
    up_weight = noise(keys[4], (EXPERTS, D, FWIN), D ** -0.5, 0.09375, ((0, 16), (2, 2)))
    down_weight = noise(keys[5], (EXPERTS, D, FWIN), FWIN ** -0.5, 0.1875, ((0, 16), (2, 2)))
    return dict(tokens=tokens, expert_ids=expert_ids, gate_values=gate_values, gate_weight=gate_weight, up_weight=up_weight, down_weight=down_weight)


def expert_apply(gathered, gate_matrix, up_matrix, down_matrix):
    gate_part = jnp.dot(gathered, gate_matrix, preferred_element_type=jnp.float32)
    up_part = jnp.dot(gathered, up_matrix, preferred_element_type=jnp.float32)
    hidden = (jax.nn.silu(gate_part) * up_part).astype(jnp.bfloat16)
    result = lax.dot_general(hidden, down_matrix, (((1,), (1,)), ((), ())), preferred_element_type=jnp.float32)
    return result.astype(jnp.bfloat16)


def reference(tokens, expert_ids, gate_values, gate_weight, up_weight, down_weight):
    blocks = TOKENS // TOK_DEV
    pair_count = TOK_DEV * TOPK
    block_ids = expert_ids.reshape(blocks, pair_count)
    onehot = (block_ids[:, :, None] == jnp.arange(EXPERTS, dtype=jnp.int32)[None, None, :]).astype(jnp.int32)
    earlier = jnp.cumsum(onehot, axis=1) - onehot
    slot_index = jnp.sum(earlier * onehot, axis=2).astype(jnp.int32)
    token_of = (jnp.arange(blocks, dtype=jnp.int32)[:, None] * TOK_DEV
                + jnp.arange(pair_count, dtype=jnp.int32)[None, :] // TOPK).astype(jnp.int32)
    block_of = jnp.broadcast_to(jnp.arange(blocks, dtype=jnp.int32)[:, None], (blocks, pair_count))
    token_table = jnp.full((EXPERTS, blocks, CAP), TOKENS, dtype=jnp.int32)
    token_table = token_table.at[block_ids, block_of, slot_index].set(token_of)
    gate_table = jnp.zeros((EXPERTS, blocks, CAP), dtype=jnp.float32)
    gate_table = gate_table.at[block_ids, block_of, slot_index].set(gate_values.reshape(blocks, pair_count))
    padded = jnp.concatenate([tokens, jnp.zeros((1, D), dtype=jnp.bfloat16)], axis=0)

    def expert_step(summed, expert):
        targets = token_table[expert].reshape(-1)
        gathered = padded[targets]
        result = expert_apply(gathered, gate_weight[expert], up_weight[expert], down_weight[expert])
        weights_here = gate_table[expert].reshape(-1)
        summed = summed.at[targets].add(weights_here[:, None] * result.astype(jnp.float32), mode="drop")
        return summed, None

    summed, unused = lax.scan(expert_step, jnp.zeros((TOKENS, D), dtype=jnp.float32), jnp.arange(EXPERTS, dtype=jnp.int32))
    return summed.astype(jnp.bfloat16)
```

```python
import jax
import jax.numpy as jnp
from jax import lax
from jax.sharding import PartitionSpec as P


def local(tokens, expert_ids, gate_values, gate_weight, up_weight, down_weight):
    groups = lax.axis_size("ep")
    experts = jnp.arange(groups, dtype=jnp.int32)
    chosen = expert_ids[:, :, None] == experts[None, None, :]
    dense_gate = jnp.sum(jnp.where(chosen, gate_values[:, :, None], 0.0), axis=1)
    gates = lax.all_to_all(dense_gate.T, "ep", split_axis=0, concat_axis=0, tiled=True)
    routed = lax.all_gather(tokens, "ep", axis=0, tiled=True)
    gate_piece = lax.all_gather(gate_weight[0], "fsdp", axis=1, tiled=True)
    up_piece = lax.all_gather(up_weight[0], "fsdp", axis=1, tiled=True)
    down_piece = lax.all_gather(down_weight[0], "fsdp", axis=1, tiled=True)
    gate_part = jnp.dot(routed, gate_piece, preferred_element_type=jnp.float32)
    up_part = jnp.dot(routed, up_piece, preferred_element_type=jnp.float32)
    hidden = (jax.nn.silu(gate_part) * up_part).astype(jnp.bfloat16)
    expert_out = lax.dot_general(
        hidden, down_piece, (((1,), (1,)), ((), ())), preferred_element_type=jnp.float32
    ).astype(jnp.bfloat16)
    weighted = (gates.reshape(-1, 1) * expert_out.astype(jnp.float32)).astype(jnp.bfloat16)
    return lax.psum_scatter(weighted, "ep", scatter_dimension=0, tiled=True)


def solution(mesh):
    placed = (
        P(("ep", "fsdp"), None),
        P(("ep", "fsdp"), None),
        P(("ep", "fsdp"), None),
        P("ep", None, "fsdp"),
        P("ep", None, "fsdp"),
        P("ep", None, "fsdp"),
    )
    return jax.shard_map(
        local, mesh=mesh, in_specs=placed, out_specs=P(("ep", "fsdp"), None), check_vma=False
    )
```

```python
import functools
import math

import jax
import jax.numpy as jnp
from jax import lax
from jax.experimental import pallas as pl
from jax.experimental.pallas import tpu as pltpu
from jax.sharding import PartitionSpec as P

MESH = pl.DeviceIdType.MESH
VMEM_LIMIT = 60 * 1024 * 1024
LANES = 128


def plain(tokens, expert_ids, gate_values, gate_weight, up_weight, down_weight):
    groups = lax.axis_size("ep")
    experts = jnp.arange(groups, dtype=jnp.int32)
    chosen = expert_ids[:, :, None] == experts[None, None, :]
    dense_gate = jnp.sum(jnp.where(chosen, gate_values[:, :, None], 0.0), axis=1)
    gates = lax.all_to_all(dense_gate.T, "ep", split_axis=0, concat_axis=0, tiled=True)
    routed = lax.all_gather(tokens, "ep", axis=0, tiled=True)
    gate_piece = lax.all_gather(gate_weight[0], "fsdp", axis=1, tiled=True)
    up_piece = lax.all_gather(up_weight[0], "fsdp", axis=1, tiled=True)
    down_piece = lax.all_gather(down_weight[0], "fsdp", axis=1, tiled=True)
    gate_part = jnp.dot(routed, gate_piece, preferred_element_type=jnp.float32)
    up_part = jnp.dot(routed, up_piece, preferred_element_type=jnp.float32)
    hidden = (jax.nn.silu(gate_part) * up_part).astype(jnp.bfloat16)
    expert_out = lax.dot_general(
        hidden, down_piece, (((1,), (1,)), ((), ())), preferred_element_type=jnp.float32
    ).astype(jnp.bfloat16)
    weighted = (gates.reshape(-1, 1) * expert_out.astype(jnp.float32)).astype(jnp.bfloat16)
    return lax.psum_scatter(weighted, "ep", scatter_dimension=0, tiled=True)


def flip(index, mask):
    bit = 1
    while bit <= mask:
        if mask & bit:
            index = index + bit * (1 - 2 * ((index // bit) % 2))
        bit *= 2
    return index


def kernel(
    groups, rows, width, units, top, pieces,
    tokens_ref, ids_ref, values_ref, gate_hbm, up_hbm, down_hbm, out_ref,
    tok, wg, wu, wd, hid, part, relay_x, relay_y, from_x, from_y, plane_sum, from_z,
    local_sem, send_sem, recv_sem,
):
    me = lax.axis_index("ep")
    core = lax.axis_index("fsdp")
    planes = list(range(0, groups, 4))
    half = width // 2
    counter = [0]

    def peer(mask):
        return (flip(me, mask), core)

    def remote(src, dst, device):
        number = counter[0]
        counter[0] += 1
        return pltpu.make_async_remote_copy(
            src_ref=src, dst_ref=dst, send_sem=send_sem.at[number], recv_sem=recv_sem.at[number],
            device_id=device, device_id_type=MESH,
        )

    def slot(ref, mask):
        return ref.at[pl.ds(mask * rows, rows)]

    def left(ref, mask):
        return ref.at[pl.ds(mask * rows, rows), pl.ds(0, half)]

    def right(ref, mask, total):
        return ref.at[pl.ds(mask * rows, rows), pl.ds(half, total - half)]

    full = width + LANES
    ends = {p: remote(slot(tok, 0), slot(tok, p), peer(p)) for p in planes[1:]}
    whole_x = {p: remote(slot(tok, p), slot(tok, p + 1), peer(1)) for p in planes}
    whole_y = {p: remote(slot(tok, p), slot(tok, p + 2), peer(2)) for p in planes}
    on_y = {p: remote(left(tok, p + 1), left(tok, p + 3), peer(2)) for p in planes}
    on_x = {p: remote(right(tok, p + 2, full), right(tok, p + 3, full), peer(1)) for p in planes}
    sibling = (me, flip(core, 1))
    other = [
        remote(gate_hbm.at[0], wg.at[1], sibling),
        remote(up_hbm.at[0], wu.at[1], sibling),
        remote(down_hbm.at[0], wd.at[1], sibling),
    ]
    diag_x, diag_y, sum_x, sum_y, sum_z = {}, {}, {}, {}, {}
    for i, p in enumerate(planes):
        diag_x[p] = remote(left(part, p + 3), slot(relay_x, i), peer(1))
        diag_y[p] = remote(right(part, p + 3, width), slot(relay_y, i), peer(2))
        sum_x[p] = remote(slot(part, p + 1), slot(from_x, i), peer(1))
        sum_y[p] = remote(slot(part, p + 2), slot(from_y, i), peer(2))
        if i:
            sum_z[p] = remote(slot(plane_sum, i), slot(from_z, i - 1), peer(p))

    barrier = pltpu.get_barrier_semaphore()
    for mask in [1, 2] + planes[1:]:
        pl.semaphore_signal(barrier, inc=1, device_id=peer(mask), device_id_type=MESH)
    pl.semaphore_signal(barrier, inc=1, device_id=sibling, device_id_type=MESH)

    own = [
        pltpu.make_async_copy(gate_hbm.at[0], wg.at[0], local_sem.at[0]),
        pltpu.make_async_copy(up_hbm.at[0], wu.at[0], local_sem.at[1]),
        pltpu.make_async_copy(down_hbm.at[0], wd.at[0], local_sem.at[2]),
    ]
    mine = pltpu.make_async_copy(tokens_ref, tok.at[pl.ds(0, rows), pl.ds(0, width)], local_sem.at[3])
    mine.start()
    for copy in own:
        copy.start()

    lane = lax.broadcasted_iota(jnp.int32, (rows, LANES), 1)
    expert = lane % groups
    dense = jnp.zeros((rows, LANES), jnp.float32)
    for k in range(top):
        dense = dense + jnp.where(ids_ref[:, k:k + 1] == expert, values_ref[:, k:k + 1], 0.0)
    piece = lane // groups
    packed, rest = jnp.zeros((rows, LANES), jnp.float32), dense
    for i in range(pieces):
        rounded = rest.astype(jnp.bfloat16).astype(jnp.float32)
        packed = jnp.where(piece == i, rounded, packed)
        rest = rest - rounded
    tok[0:rows, width:full] = packed.astype(jnp.bfloat16)

    mine.wait()
    pl.semaphore_wait(barrier, 2 + len(planes))

    for p in planes[1:3]:
        ends[p].start()
    whole_x[0].start()
    whole_y[0].start()
    for copy in other:
        copy.start()

    block = 4 * rows
    step = math.gcd(units, 256)

    def gate_up(p, h):
        def body(j, carry):
            columns = pl.ds(pl.multiple_of(j * step, step), step)
            x = tok[p * rows:p * rows + block, 0:width]
            g = jnp.dot(x, wg[h, :, columns], preferred_element_type=jnp.float32)
            u = jnp.dot(x, wu[h, :, columns], preferred_element_type=jnp.float32)
            hid[h, :, columns] = (g / (1.0 + jnp.exp(-g)) * u).astype(jnp.bfloat16)
            return carry

        lax.fori_loop(0, units // step, body, 0)

    def down(p):
        lanes = lax.broadcasted_iota(jnp.int32, (block, LANES), 1)
        shown = tok[p * rows:p * rows + block, width:full].astype(jnp.float32)
        gate = jnp.sum(jnp.where(lanes % groups == me, shown, 0.0), axis=1, keepdims=True)
        wide = math.gcd(width, 512)

        def body(n, carry):
            features = pl.ds(pl.multiple_of(n * wide, wide), wide)
            total = None
            for h in range(2):
                term = lax.dot_general(
                    hid[h], wd[h, features, :], (((1,), (1,)), ((), ())),
                    preferred_element_type=jnp.float32,
                )
                total = term if total is None else total + term
            rounded = total.astype(jnp.bfloat16).astype(jnp.float32)
            part[p * rows:p * rows + block, features] = (gate * rounded).astype(jnp.bfloat16)
            return carry

        lax.fori_loop(0, width // wide, body, 0)

    def add_relays(p):
        i = p // 4
        here = slice(i * rows, (i + 1) * rows)
        diag_x[p].wait_recv()
        diag_y[p].wait_recv()
        to_y = slice((p + 2) * rows, (p + 3) * rows)
        to_x = slice((p + 1) * rows, (p + 2) * rows)
        part[to_y, 0:half] = (
            part[to_y, 0:half].astype(jnp.float32) + relay_x[here].astype(jnp.float32)
        ).astype(jnp.bfloat16)
        part[to_x, half:width] = (
            part[to_x, half:width].astype(jnp.float32) + relay_y[here].astype(jnp.float32)
        ).astype(jnp.bfloat16)
        sum_x[p].start()
        sum_y[p].start()

    def finish_plane(p):
        i = p // 4
        here = slice(i * rows, (i + 1) * rows)
        sum_x[p].wait_recv()
        sum_y[p].wait_recv()
        total = (
            part[p * rows:(p + 1) * rows].astype(jnp.float32)
            + from_x[here].astype(jnp.float32)
            + from_y[here].astype(jnp.float32)
        )
        if i:
            plane_sum[here] = total.astype(jnp.bfloat16)
            sum_z[p].start()
        return total

    order = []
    for i, p in enumerate(planes):
        whole_x[p].wait_recv()
        on_y[p].start()
        whole_y[p].wait_recv()
        on_x[p].start()
        if i == 0:
            for q in planes[3:]:
                ends[q].start()
        if i + 1 < len(planes):
            following = planes[i + 1]
            ends[following].wait_recv()
            whole_x[following].start()
            whole_y[following].start()
        on_y[p].wait_recv()
        on_x[p].wait_recv()
        if i == 0:
            own[0].wait()
            own[1].wait()
        gate_up(p, 0)
        if i == 0:
            other[0].wait_recv()
            other[1].wait_recv()
        gate_up(p, 1)
        if i == 0:
            own[2].wait()
            other[2].wait_recv()
        down(p)
        if i:
            diag_x[p].start()
            diag_y[p].start()
            order.append(p)
        if len(order) >= 2:
            add_relays(order[-2])
        if len(order) >= 3:
            finish_plane(order[-3])
    diag_x[0].start()
    diag_y[0].start()
    order.append(0)
    count = len(order)
    finish_plane(order[count - 3])
    add_relays(order[count - 2])
    add_relays(order[count - 1])
    finish_plane(order[count - 2])
    total = finish_plane(order[count - 1])
    for i, p in enumerate(planes[1:]):
        sum_z[p].wait_recv()
        total = total + from_z[i * rows:(i + 1) * rows].astype(jnp.float32)
    out_ref[...] = total.astype(jnp.bfloat16)

    for group in (ends, whole_x, whole_y, on_y, on_x, diag_x, diag_y, sum_x, sum_y, sum_z):
        for copy in group.values():
            copy.wait_send()
    for copy in other:
        copy.wait_send()


def fused(tokens, expert_ids, gate_values, gate_weight, up_weight, down_weight):
    rows, width = tokens.shape
    units = gate_weight.shape[2]
    top = expert_ids.shape[1]
    groups = lax.axis_size("ep")
    planes = groups // 4
    half = width // 2
    copies = 3 + (planes - 1) * 2 + planes * 8
    bf16 = jnp.bfloat16
    run = pl.pallas_call(
        functools.partial(kernel, groups, rows, width, units, top, 3),
        out_shape=jax.ShapeDtypeStruct((rows, width), bf16),
        in_specs=[
            pl.BlockSpec(memory_space=pl.ANY),
            pl.BlockSpec(memory_space=pltpu.VMEM),
            pl.BlockSpec(memory_space=pltpu.VMEM),
            pl.BlockSpec(memory_space=pl.ANY),
            pl.BlockSpec(memory_space=pl.ANY),
            pl.BlockSpec(memory_space=pl.ANY),
        ],
        out_specs=pl.BlockSpec(memory_space=pltpu.VMEM),
        scratch_shapes=[
            pltpu.VMEM((groups * rows, width + LANES), bf16),
            pltpu.VMEM((2, width, units), bf16),
            pltpu.VMEM((2, width, units), bf16),
            pltpu.VMEM((2, width, units), bf16),
            pltpu.VMEM((2, 4 * rows, units), bf16),
            pltpu.VMEM((groups * rows, width), bf16),
            pltpu.VMEM((planes * rows, half), bf16),
            pltpu.VMEM((planes * rows, width - half), bf16),
            pltpu.VMEM((planes * rows, width), bf16),
            pltpu.VMEM((planes * rows, width), bf16),
            pltpu.VMEM((planes * rows, width), bf16),
            pltpu.VMEM(((planes - 1) * rows, width), bf16),
            pltpu.SemaphoreType.DMA((4,)),
            pltpu.SemaphoreType.DMA((copies,)),
            pltpu.SemaphoreType.DMA((copies,)),
        ],
        compiler_params=pltpu.CompilerParams(
            collective_id=0, has_side_effects=True, vmem_limit_bytes=VMEM_LIMIT
        ),
        cost_estimate=pl.CostEstimate(
            flops=12 * groups * rows * width * units, bytes_accessed=6 * width * units, transcendentals=0
        ),
    )
    return run(tokens, expert_ids, gate_values, gate_weight, up_weight, down_weight)


def solution(mesh):
    placed = (
        P(("ep", "fsdp"), None),
        P(("ep", "fsdp"), None),
        P(("ep", "fsdp"), None),
        P("ep", None, "fsdp"),
        P("ep", None, "fsdp"),
        P("ep", None, "fsdp"),
    )
    groups, cores = mesh.shape["ep"], mesh.shape["fsdp"]

    def local(tokens, expert_ids, gate_values, gate_weight, up_weight, down_weight):
        rows, width = tokens.shape
        units = gate_weight.shape[2]
        held = 2 * (6 * width * units + 4 * rows * 2 * units)
        held += 2 * rows * width * (2 * groups + groups)
        fits = held + VMEM_LIMIT // 6 <= VMEM_LIMIT
        shaped = (
            cores == 2 and groups >= 16 and groups & (groups - 1) == 0 and 3 * groups <= LANES
            and rows % 16 == 0 and width % 256 == 0 and units % 128 == 0
        )
        part = fused if fits and shaped else plain
        return part(tokens, expert_ids, gate_values, gate_weight, up_weight, down_weight)

    return jax.shard_map(
        local, mesh=mesh, in_specs=placed, out_specs=P(("ep", "fsdp"), None), check_vma=False
    )
```
